32 devices in a mesh: section: 8 (over y, x, core), sp: 4 (over z).
Axes of the slice: x: 2, y: 2, z: 4, core: 2. Of those that a mesh axis runs over, the one named last changes fastest.
Arguments:
- resid: float32 [8, 896, 6144], P('section', 'sp'), may hold values from -1.8 to 1.8
- qkv: bfloat16 [8, 896, 3, 6144], P('section', 'sp'), may hold values from -48 to 48
- cache_kv: bfloat16 [8, 2, 2, 1344, 6144], P('section', None, None, None, 'sp'), may hold values from -6 to 6
- out_proj: bfloat16 [8, 6144, 6144], P('section', 'sp'), may hold values from -0.078125 to 0.078125
- gate: float32 [8, 2, 6144], P('section'), may hold values from 0.5 to 2
- span_ids: int32 [8], P('section'), may hold values from 3 to 39
- cache_counts: int32 [8], P('section'), may hold values from 0 to 3, as said below
- span_mask: int32 [40, 40], replicated, may hold values from 0 to 1, as said below
Outputs:
- carried: float32 [8, 896, 6144], P('section', 'sp')
The draws below stay inside these ranges and needn't reach their ends.
Inputs may be any that keep to these rules, and one draw needn't show every extreme that they name: `cache_counts`: some section has all 3 slots filled. span_mask[i][j] is 0 for j > i and 1 for j = i.
All inputs are finite; a program needn't handle non-finite values.
Results may differ from the reference program's by a relative error of at most 0.006.
Values may be sent and summed in bfloat16 or wider, within the bound.
A program may use at most 384 MiB of HBM per device.

```python
import jax
import jax.numpy as jnp
from jax import lax

D = 6144
HEADS = 48
HDIM = 128
SPAN = 448
NCHUNK = 40
SLOTS = 3
VIDS = 2
SECTIONS = 8
TOKS = 896
HD = 6144
KEYS = 1344


def draw_qkv(key, part):
    key_base = jax.random.fold_in(key, 0)
    shape = (SECTIONS, TOKS, 3, HD)
    channel = jnp.array([2.0, 1.0, 1.0], jnp.float32)[None, None, :, None]
    result = jnp.clip(jax.random.normal(key_base, shape, jnp.float32), -6.0, 6.0) * channel
    return result.astype(jnp.bfloat16)


def draw_cache_counts(key, part):
    key_fill, key_full = jax.random.split(key)
    filled = jax.random.randint(key_fill, (SECTIONS,), 0, SLOTS + 1, dtype=jnp.int32)
    fullest = jax.random.randint(key_full, (), 0, SECTIONS, dtype=jnp.int32)
    return jnp.where(jnp.arange(SECTIONS, dtype=jnp.int32) == fullest, SLOTS, filled).astype(jnp.int32)


def draw_span_mask(key, part):
    coins = jax.random.randint(key, (NCHUNK, NCHUNK), 0, 4, dtype=jnp.int32)
    row_index = jnp.arange(NCHUNK, dtype=jnp.int32)[:, None]
    col_index = jnp.arange(NCHUNK, dtype=jnp.int32)[None, :]
    earlier = jnp.where(coins > 0, 1, 0)
    return jnp.where(col_index < row_index, earlier, jnp.where(col_index == row_index, 1, 0)).astype(jnp.int32)


def with_ends(values, own_key, low, high):
    extent = values.shape
    place = [jax.random.randint(jax.random.fold_in(own_key, axis), (), 0, extent[axis]) for axis in range(len(extent))]
    values = values.at[tuple(place)].set(low)
    longest = extent.index(max(extent))
    place[longest] = (place[longest] + 1) % extent[longest]
    return values.at[tuple(place)].set(high)


def level_of(stream_key, extent, shards, low, top_value):
    def one(axis_at, blocks):
        heights = jax.random.uniform(jax.random.fold_in(jax.random.fold_in(stream_key, 6), axis_at), (blocks,), jnp.float32, low / len(shards), top_value / len(shards))
        return jnp.repeat(jnp.exp(heights), extent[axis_at] // blocks).reshape((-1,) + (1,) * (len(extent) - axis_at - 1))

    factor_of = one(*shards[0])
    for cut in shards[1:]:
        factor_of = factor_of * one(*cut)
    return factor_of


def centred(rng, extent, width, limit, shards=(), kind=jnp.bfloat16):
    factor_of = level_of(rng, extent, shards, -0.22, 0.18) if shards else 1.0
    values = jax.random.normal(rng, extent, jnp.float32) * width * factor_of
    return jnp.minimum(jnp.maximum(values, -limit), limit).astype(kind)


def setup_inputs(seed: int = 0) -> dict:
    splits = jax.random.split(jax.random.key(seed), 9)
    resid = centred(splits[0], (SECTIONS, TOKS, D), 0.3, 1.8, ((0, 8), (1, 4)), jnp.float32)
    qkv = draw_qkv(jax.random.fold_in(splits[8], 71), 0)
    cache_kv = centred(splits[2], (SECTIONS, 2, VIDS, KEYS, HD), 1.0, 6.0, ((0, 8), (4, 4)))
    out_proj = centred(splits[3], (SECTIONS, HD, D), HD ** -0.5, 0.078125, ((0, 8), (1, 4)))
    gate = jnp.clip(0.5 + 1.5 * jax.random.uniform(splits[4], (SECTIONS, VIDS, D), jnp.float32) ** level_of(splits[4], (SECTIONS, VIDS, D), ((0, 8),), -0.2, 0.2), 0.5, 2.0)
    span_ids = with_ends(jax.random.randint(splits[5], (SECTIONS,), SLOTS, NCHUNK), jax.random.fold_in(splits[5], 1), SLOTS, NCHUNK - 1).astype(jnp.int32)
    cache_counts = draw_cache_counts(jax.random.fold_in(splits[8], 71), 0)
    span_mask = draw_span_mask(jax.random.fold_in(splits[8], 71), 0)
    return {"resid": resid, "qkv": qkv, "cache_kv": cache_kv, "out_proj": out_proj, "gate": gate, "span_ids": span_ids, "cache_counts": cache_counts, "span_mask": span_mask}


def visible_slots(span_id, filled, span_mask):
    row_mask = lax.dynamic_index_in_dim(span_mask, span_id, 0, keepdims=False)
    slot_ids = jnp.arange(SLOTS, dtype=jnp.int32)
    wanted = span_id - 1 - slot_ids
    columns = jnp.arange(NCHUNK, dtype=jnp.int32)
    looked = jnp.sum(jnp.where(columns[None, :] == wanted[:, None], row_mask[None, :], 0), axis=1)
    return (slot_ids < filled) & (looked == 1)


def attend(queries, own_keys, own_values, cache_keys, cache_values, key_live):
    score_scale = HDIM ** -0.5
    keys_all = jnp.concatenate([cache_keys, own_keys], axis=0).astype(jnp.float32)
    values_all = jnp.concatenate([cache_values, own_values], axis=0).astype(jnp.float32)
    scores = jnp.einsum("qhe,khe->hqk", queries.astype(jnp.float32), keys_all) * score_scale
    live_all = jnp.concatenate([key_live, jnp.ones((SPAN,), dtype=bool)])
    scores = jnp.where(live_all[None, None, :], scores, -jnp.inf)
    highest = jnp.max(scores, axis=2, keepdims=True)
    raised = jnp.exp(scores - highest)
    weights = (raised / jnp.sum(raised, axis=2, keepdims=True)).astype(jnp.bfloat16)
    mixed = jnp.einsum("hqk,khe->qhe", weights.astype(jnp.float32), values_all)
    return mixed.astype(jnp.bfloat16).reshape(SPAN, HD)


def reference(resid, qkv, cache_kv, out_proj, gate, span_ids, cache_counts, span_mask):
    def one_section(inputs_one):
        resid_one, qkv_one, cache_one, proj_one, gate_one, span_id, filled = inputs_one
        live_slots = visible_slots(span_id, filled, span_mask)
        key_live = jnp.repeat(live_slots, SPAN)
        split_rows = qkv_one.reshape(VIDS, SPAN, 3, HEADS, HDIM)
        cache_keys = cache_one[0].reshape(VIDS, KEYS, HEADS, HDIM)
        cache_values = cache_one[1].reshape(VIDS, KEYS, HEADS, HDIM)

        def one_video(video_in):
            return attend(video_in[0], video_in[1], video_in[2], video_in[3], video_in[4], key_live)

        heads_out = lax.map(one_video, (split_rows[:, :, 0], split_rows[:, :, 1], split_rows[:, :, 2], cache_keys, cache_values))
        heads_out = heads_out.reshape(TOKS, HD)
        projected = jnp.dot(heads_out, proj_one, preferred_element_type=jnp.float32)
        video_of = jnp.arange(TOKS, dtype=jnp.int32) // SPAN
        return resid_one + gate_one[video_of] * projected

    layer_out = lax.map(one_section, (resid, qkv, cache_kv, out_proj, gate, span_ids, cache_counts))
    return jnp.roll(layer_out, 1, axis=0)
```

```python
import math

import jax
import jax.numpy as jnp
from jax import lax
from jax.experimental import pallas as pl
from jax.experimental.pallas import tpu as pltpu
from jax.sharding import PartitionSpec as P

HDIM = 128
SPAN = 448
NCHUNK = 40
SLOTS = 3
VIDS = 2
TOKS = 896
KEYS = 1344
PAIR = 2 * HDIM
FLOOR = -3.0e38
SCALE = HDIM ** (-0.5) * math.log2(math.e)
COLS = 1024


def swapped(shard, axis, bit):
    devices = lax.axis_size(axis)
    return lax.ppermute(shard, axis, [(i, i ^ bit) for i in range(devices)])


def passed_along(shard, axis, by):
    devices = lax.axis_size(axis)
    return lax.ppermute(shard, axis, [(i, (i + by) % devices) for i in range(devices)])


def visible_slots(span_id, filled, span_mask):
    row_mask = lax.dynamic_index_in_dim(span_mask, span_id, 0, keepdims=False)
    slot_ids = jnp.arange(SLOTS, dtype=jnp.int32)
    wanted = span_id - 1 - slot_ids
    columns = jnp.arange(NCHUNK, dtype=jnp.int32)
    looked = jnp.sum(jnp.where(columns[None, :] == wanted[:, None], row_mask[None, :], 0), axis=1)
    return (slot_ids < filled) & (looked == 1)


def dot_t(left, right):
    return lax.dot_general(left, right, (((1,), (1,)), ((), ())), preferred_element_type=jnp.float32)


def far_kernel(q_ref, k_ref, v_ref, bias_ref, acc_ref, stat_ref):
    for head in range(2):
        cols = slice(head * HDIM, (head + 1) * HDIM)
        scores = dot_t(q_ref[:, cols], k_ref[0, 0, 0, :, cols]) + bias_ref[0:1, :]
        highest = jnp.maximum(jnp.max(scores, axis=1, keepdims=True), FLOOR)
        raised = jnp.exp2(scores * SCALE - highest * SCALE)
        total = jnp.sum(raised, axis=1, keepdims=True)
        acc_ref[:, cols] = jnp.dot(
            raised.astype(jnp.bfloat16), v_ref[0, 0, 0, :, cols], preferred_element_type=jnp.float32
        )
        lane = lax.broadcasted_iota(jnp.int32, (SPAN, HDIM), 1)
        stat_ref[:, cols] = jnp.where(lane < HDIM // 2, highest, total)


def near_kernel(q_ref, k_ref, v_ref, acc_ref, stat_ref, out_ref):
    for head in range(2):
        cols = slice(head * HDIM, (head + 1) * HDIM)
        scores = dot_t(q_ref[:, cols], k_ref[:, cols])
        far_high = stat_ref[:, head * HDIM : head * HDIM + 1]
        far_total = stat_ref[:, head * HDIM + HDIM // 2 : head * HDIM + HDIM // 2 + 1]
        highest = jnp.maximum(jnp.max(scores, axis=1, keepdims=True), far_high)
        raised = jnp.exp2(scores * SCALE - highest * SCALE)
        fade = jnp.exp2((far_high - highest) * SCALE)
        total = jnp.sum(raised, axis=1, keepdims=True) + far_total * fade
        mixed = jnp.dot(raised.astype(jnp.bfloat16), v_ref[:, cols], preferred_element_type=jnp.float32)
        mixed = (mixed + acc_ref[:, cols] * fade) / total
        out_ref[:, cols] = mixed.astype(jnp.bfloat16)


def far_mix(queries, cache_kv, live_slots):
    width = queries.shape[1]
    bias = jnp.where(jnp.repeat(live_slots, SPAN), 0.0, -jnp.inf).astype(jnp.float32)
    bias = jnp.broadcast_to(bias[None, :], (8, KEYS))
    block = pl.BlockSpec((SPAN, PAIR), lambda b, h: (b, h))
    return pl.pallas_call(
        far_kernel,
        grid=(VIDS, width // PAIR),
        in_specs=[
            block,
            pl.BlockSpec((1, 1, 1, KEYS, PAIR), lambda b, h: (0, 0, b, 0, h)),
            pl.BlockSpec((1, 1, 1, KEYS, PAIR), lambda b, h: (0, 1, b, 0, h)),
            pl.BlockSpec((8, KEYS), lambda b, h: (0, 0)),
        ],
        out_specs=[block, block],
        out_shape=[jax.ShapeDtypeStruct((TOKS, width), jnp.float32)] * 2,
        compiler_params=pltpu.CompilerParams(vmem_limit_bytes=40 * 1024 * 1024),
        cost_estimate=pl.CostEstimate(
            flops=4 * TOKS * KEYS * width * 4,
            bytes_accessed=2 * VIDS * KEYS * width * 2 + TOKS * width * 10,
            transcendentals=TOKS * KEYS * (width // HDIM),
        ),
    )(queries, cache_kv, cache_kv, bias)


def near_mix(queries, keys, values, acc, stat):
    width = queries.shape[1]
    block = pl.BlockSpec((SPAN, PAIR), lambda b, h: (b, h))
    return pl.pallas_call(
        near_kernel,
        grid=(VIDS, width // PAIR),
        in_specs=[block] * 5,
        out_specs=block,
        out_shape=jax.ShapeDtypeStruct((TOKS, width), jnp.bfloat16),
        compiler_params=pltpu.CompilerParams(vmem_limit_bytes=40 * 1024 * 1024),
        cost_estimate=pl.CostEstimate(
            flops=4 * TOKS * SPAN * width * 4,
            bytes_accessed=TOKS * width * 16,
            transcendentals=TOKS * SPAN * (width // HDIM),
        ),
    )(queries, keys, values, acc, stat)


def heads_gathered(local, place, devices):
    rows, width = local.shape[0], local.shape[1] // devices
    whole = jnp.zeros((rows * devices, width), local.dtype)
    for bit in range(devices):
        other = place ^ bit
        piece = lax.dynamic_slice(local, (0, other * width), (rows, width))
        if bit:
            piece = swapped(piece, "sp", bit)
        whole = lax.dynamic_update_slice(whole, piece, (other * rows, 0))
    return whole


def per_device(resid, qkv, cache_kv, out_proj, gate, span_ids, cache_counts, span_mask):
    own_rows = resid.shape[1]
    model = resid.shape[2]
    devices = lax.axis_size("sp")
    place = lax.axis_index("sp")
    live_slots = visible_slots(span_ids[0], cache_counts[0], span_mask)

    queries = heads_gathered(qkv[0, :, 0], place, devices)
    acc, stat = far_mix(queries, cache_kv, live_slots)
    keys = heads_gathered(qkv[0, :, 1], place, devices)
    values = heads_gathered(qkv[0, :, 2], place, devices)
    heads_all = near_mix(queries, keys, values, acc, stat)

    resid_prev = passed_along(resid[0], "section", 1)
    gate_prev = passed_along(gate[0], "section", 1)
    video_of = (place * own_rows + jnp.arange(own_rows, dtype=jnp.int32)) // SPAN

    row_blocks = [
        lax.dynamic_slice(heads_all, ((place ^ bit) * own_rows, 0), (own_rows, heads_all.shape[1]))
        for bit in range(devices)
    ]
    odd = jnp.concatenate(row_blocks[1::2], axis=0)
    even = jnp.concatenate(row_blocks[0::2], axis=0)
    pieces = []
    for start in range(0, model, COLS):
        proj = out_proj[0, :, start : start + COLS]
        sent = jnp.dot(odd, proj, preferred_element_type=jnp.float32).astype(jnp.bfloat16)
        summed = jnp.dot(even, proj, preferred_element_type=jnp.float32)
        summed = summed + swapped(sent, "sp", 1).astype(jnp.float32)
        blocks = [summed[i * own_rows : (i + 1) * own_rows] for i in range(devices // 2)]
        bit = 2
        while bit < devices:
            sent = jnp.concatenate(blocks[1::2], axis=0).astype(jnp.bfloat16)
            arrived = swapped(sent, "sp", bit).astype(jnp.float32)
            kept = blocks[0::2]
            blocks = [kept[i] + arrived[i * own_rows : (i + 1) * own_rows] for i in range(len(kept))]
            bit *= 2
        moved = passed_along(blocks[0].astype(jnp.bfloat16), "section", 1).astype(jnp.float32)
        gate_cols = gate_prev[:, start : start + COLS]
        gains = jnp.where((video_of == 0)[:, None], gate_cols[0:1], gate_cols[1:2])
        pieces.append(resid_prev[:, start : start + COLS] + gains * moved)
    return jnp.concatenate(pieces, axis=1)[None]


def solution(mesh):
    in_specs = (
        P("section", "sp", None),
        P("section", "sp", None, None),
        P("section", None, None, None, "sp"),
        P("section", "sp", None),
        P("section", None, None),
        P("section"),
        P("section"),
        P(),
    )
    out_specs = P("section", "sp", None)
    return jax.shard_map(
        per_device, mesh=mesh, in_specs=in_specs, out_specs=out_specs, check_vma=False
    )
```

```python
import math

import jax
import jax.numpy as jnp
from jax import lax
from jax.experimental import pallas as pl
from jax.experimental.pallas import tpu as pltpu
from jax.sharding import PartitionSpec as P

HDIM = 128
SPAN = 448
NCHUNK = 40
SLOTS = 3
VIDS = 2
TOKS = 896
KEYS = 1344
PAIR = 2 * HDIM
FLOOR = -3.0e38
SCALE = HDIM ** (-0.5) * math.log2(math.e)
COLS = 512
LAG = 2


def swapped(shard, axis, bit):
    devices = lax.axis_size(axis)
    return lax.ppermute(shard, axis, [(i, i ^ bit) for i in range(devices)])


def passed_along(shard, axis, by):
    devices = lax.axis_size(axis)
    return lax.ppermute(shard, axis, [(i, (i + by) % devices) for i in range(devices)])


def visible_slots(span_id, filled, span_mask):
    row_mask = lax.dynamic_index_in_dim(span_mask, span_id, 0, keepdims=False)
    slot_ids = jnp.arange(SLOTS, dtype=jnp.int32)
    wanted = span_id - 1 - slot_ids
    columns = jnp.arange(NCHUNK, dtype=jnp.int32)
    looked = jnp.sum(jnp.where(columns[None, :] == wanted[:, None], row_mask[None, :], 0), axis=1)
    return (slot_ids < filled) & (looked == 1)


def dot_t(left, right):
    return lax.dot_general(left, right, (((1,), (1,)), ((), ())), preferred_element_type=jnp.float32)


def far_kernel(q_ref, k_ref, v_ref, bias_ref, acc_ref, high_ref, total_ref):
    for head in range(2):
        cols = slice(head * HDIM, (head + 1) * HDIM)
        scores = dot_t(q_ref[:, cols], k_ref[0, 0, 0, :, cols]) + bias_ref[0:1, :]
        highest = jnp.maximum(jnp.max(scores, axis=1, keepdims=True), FLOOR)
        raised = jnp.exp2(scores * SCALE - highest * SCALE)
        total = jnp.sum(raised, axis=1, keepdims=True)
        acc_ref[:, cols] = jnp.dot(
            raised.astype(jnp.bfloat16), v_ref[0, 0, 0, :, cols], preferred_element_type=jnp.float32
        )
        high_ref[:, cols] = jnp.broadcast_to(highest, (SPAN, HDIM))
        total_ref[:, cols] = jnp.broadcast_to(total, (SPAN, HDIM))


def near_kernel(q_ref, k_ref, v_ref, acc_ref, high_ref, total_ref, *rest):
    out_ref = rest[-1]
    for head in range(2):
        cols = slice(head * HDIM, (head + 1) * HDIM)
        scores = dot_t(q_ref[:, cols], k_ref[0, :, cols])
        far_high = high_ref[:, cols]
        near_high = jnp.broadcast_to(jnp.max(scores, axis=1, keepdims=True), (SPAN, HDIM))
        highest = jnp.maximum(near_high, far_high) * SCALE
        wide = jnp.concatenate([highest] * -(-SPAN // HDIM), axis=1)[:, :SPAN]
        raised = jnp.exp2(scores * SCALE - wide)
        fade = jnp.exp2(far_high * SCALE - highest)
        near_total = jnp.broadcast_to(jnp.sum(raised, axis=1, keepdims=True), (SPAN, HDIM))
        total = near_total + total_ref[:, cols] * fade
        mixed = jnp.dot(raised.astype(jnp.bfloat16), v_ref[0, :, cols], preferred_element_type=jnp.float32)
        mixed = (mixed + acc_ref[:, cols] * fade) / total
        out_ref[:, cols] = mixed.astype(jnp.bfloat16)


def far_mix(queries, cache_kv, live_slots):
    width = queries.shape[1]
    bias = jnp.where(jnp.repeat(live_slots, SPAN), 0.0, -jnp.inf).astype(jnp.float32)
    bias = jnp.broadcast_to(bias[None, :], (8, KEYS))
    block = pl.BlockSpec((SPAN, PAIR), lambda b, h: (b, h))
    return pl.pallas_call(
        far_kernel,
        grid=(VIDS, width // PAIR),
        in_specs=[
            block,
            pl.BlockSpec((1, 1, 1, KEYS, PAIR), lambda b, h: (0, 0, b, 0, h)),
            pl.BlockSpec((1, 1, 1, KEYS, PAIR), lambda b, h: (0, 1, b, 0, h)),
            pl.BlockSpec((8, KEYS), lambda b, h: (0, 0)),
        ],
        out_specs=[block] * 3,
        out_shape=[jax.ShapeDtypeStruct((TOKS, width), jnp.float32)] * 3,
        compiler_params=pltpu.CompilerParams(vmem_limit_bytes=40 * 1024 * 1024),
        cost_estimate=pl.CostEstimate(
            flops=4 * TOKS * KEYS * width * 4,
            bytes_accessed=2 * VIDS * KEYS * width * 2 + TOKS * width * 14,
            transcendentals=TOKS * KEYS * (width // HDIM),
        ),
    )(queries, cache_kv, cache_kv, bias)


def near_mix(queries, own_kv, far_parts, first, earlier):
    width, group = queries.shape[1], own_kv.shape[2]
    block = pl.BlockSpec((SPAN, PAIR), lambda b, h: (b, h + first))
    operands = [queries, own_kv, own_kv, *far_parts]
    in_specs = [
        block,
        pl.BlockSpec((1, SPAN, PAIR), lambda b, h: (0, b, h)),
        pl.BlockSpec((1, SPAN, PAIR), lambda b, h: (1, b, h)),
        block,
        block,
        block,
    ]
    aliases = {}
    if earlier is not None:
        aliases = {len(operands): 0}
        operands.append(earlier)
        in_specs.append(pl.BlockSpec(memory_space=pl.ANY))
    return pl.pallas_call(
        near_kernel,
        grid=(VIDS, group // PAIR),
        in_specs=in_specs,
        out_specs=block,
        out_shape=jax.ShapeDtypeStruct((TOKS, width), jnp.bfloat16),
        input_output_aliases=aliases,
        compiler_params=pltpu.CompilerParams(vmem_limit_bytes=40 * 1024 * 1024),
        cost_estimate=pl.CostEstimate(
            flops=4 * TOKS * SPAN * group * 4,
            bytes_accessed=TOKS * group * 20,
            transcendentals=TOKS * SPAN * (group // HDIM),
        ),
    )(*operands)


def flipped(place, bits):
    bit = 1
    while bit <= bits:
        if bits & bit:
            place = place + bit - 2 * bit * lax.rem(lax.div(place, bit), 2)
        bit *= 2
    return place


def sum_kernel(devices, heads_ref, proj_ref, out_ref, w_buf, acc, *rest):
    stages = devices.bit_length() - 1
    sends, lands = rest[: stages + 1], rest[stages + 1 : 2 * stages + 1]
    w_sem, send_sem, recv_sem = rest[2 * stages + 1 :]
    place, section = lax.axis_index("sp"), lax.axis_index("section")
    sections = lax.axis_size("section")
    after = lax.rem(section + 1, sections)
    before = lax.rem(section + sections - 1, sections)
    rows = heads_ref.shape[0] // devices
    chunks = acc.shape[0]
    cols = acc.shape[2]
    mesh_id = pl.DeviceIdType.MESH
    partners = [(section, flipped(place, 1 << k)) for k in range(stages)]

    barrier = pltpu.get_barrier_semaphore()
    for other in partners + [(before, place)]:
        pl.semaphore_signal(barrier, inc=1, device_id=other, device_id_type=mesh_id)
    pl.semaphore_wait(barrier, stages + 1)

    def columns(t):
        return pl.ds(pl.multiple_of(t * cols, cols), cols)

    def fetch(t):
        slot = lax.rem(t, 2)
        return pltpu.make_async_copy(proj_ref.at[0, :, columns(t)], w_buf.at[slot], w_sem.at[slot])

    def move(k, t):
        return pltpu.make_async_remote_copy(
            src_ref=sends[k].at[t],
            dst_ref=lands[k].at[t] if k < stages else out_ref.at[:, columns(t)],
            send_sem=send_sem.at[k, t],
            recv_sem=recv_sem.at[k, t],
            device_id=partners[k] if k < stages else (after, place),
            device_id_type=mesh_id,
        )

    def product(t, flips):
        start = pl.multiple_of(flipped(place, flips) * rows, 16)
        return jnp.dot(
            heads_ref[pl.ds(start, rows), :], w_buf[lax.rem(t, 2)], preferred_element_type=jnp.float32
        )

    def multiply(t):
        fetch(t).wait()

        @pl.when(t + 1 < chunks)
        def _():
            fetch(t + 1).start()

        for i in range(devices // 2):
            sends[0][t, i * rows : (i + 1) * rows] = product(t, 2 * i + 1).astype(jnp.bfloat16)
        move(0, t).start()
        for i in range(devices // 2):
            acc[t, i * rows : (i + 1) * rows] = product(t, 2 * i)

    def combine(k, t):
        move(k, t).wait_recv()
        count = devices >> (k + 1)
        for i in range(count):
            spot = i << k
            summed = acc[t, spot * rows : (spot + 1) * rows] + lands[k][
                t, i * rows : (i + 1) * rows
            ].astype(jnp.float32)
            if i % 2 or count == 1:
                j = i // 2
                sends[k + 1][t, j * rows : (j + 1) * rows] = summed.astype(jnp.bfloat16)
            else:
                acc[t, spot * rows : (spot + 1) * rows] = summed
        move(k + 1, t).start()

    fetch(0).start()

    def step(t, carry):
        @pl.when(t < chunks)
        def _():
            multiply(t)

        for k in range(stages):
            done = t - LAG * (k + 1)

            @pl.when((done >= 0) & (done < chunks))
            def _():
                combine(k, done)

        return carry

    lax.fori_loop(0, chunks + LAG * stages, step, 0)

    def finish(t, carry):
        move(stages, t).wait_recv()
        for k in range(stages + 1):
            move(k, t).wait_send()
        return carry

    lax.fori_loop(0, chunks, finish, 0)


def summed_and_moved(heads_all, out_proj, devices):
    width, model = out_proj.shape[1], out_proj.shape[2]
    rows = TOKS // devices
    chunks = model // COLS
    stages = devices.bit_length() - 1
    sizes = [max(devices >> (k + 1), 1) * rows for k in range(stages + 1)]
    return pl.pallas_call(
        lambda *refs: sum_kernel(devices, *refs),
        out_shape=jax.ShapeDtypeStruct((rows, model), jnp.bfloat16),
        in_specs=[pl.BlockSpec(memory_space=pltpu.VMEM), pl.BlockSpec(memory_space=pl.ANY)],
        out_specs=pl.BlockSpec(memory_space=pl.ANY),
        scratch_shapes=[
            pltpu.VMEM((2, width, COLS), jnp.bfloat16),
            pltpu.VMEM((chunks, sizes[0], COLS), jnp.float32),
        ]
        + [pltpu.VMEM((chunks, size, COLS), jnp.bfloat16) for size in sizes]
        + [pltpu.VMEM((chunks, size, COLS), jnp.bfloat16) for size in sizes[:-1]]
        + [
            pltpu.SemaphoreType.DMA((2,)),
            pltpu.SemaphoreType.DMA((stages + 1, chunks)),
            pltpu.SemaphoreType.DMA((stages + 1, chunks)),
        ],
        compiler_params=pltpu.CompilerParams(
            collective_id=0, has_side_effects=True, vmem_limit_bytes=58 * 1024 * 1024
        ),
        cost_estimate=pl.CostEstimate(
            flops=2 * TOKS * width * model, bytes_accessed=2 * width * model, transcendentals=0
        ),
    )(heads_all, out_proj)


def heads_gathered(cut, rows, place, devices):
    piece = cut(place)
    whole = jnp.zeros(piece.shape[:-2] + (rows * devices, piece.shape[-1]), piece.dtype)
    lead = (0,) * (piece.ndim - 2)
    for bit in range(devices):
        other = place ^ bit
        piece = cut(other)
        if bit:
            piece = swapped(piece, "sp", bit)
        whole = lax.dynamic_update_slice(whole, piece, (*lead, other * rows, 0))
    return whole


def per_device(resid, qkv, cache_kv, out_proj, gate, span_ids, cache_counts, span_mask):
    own_rows = resid.shape[1]
    width = cache_kv.shape[4]
    devices = lax.axis_size("sp")
    place = lax.axis_index("sp")
    live_slots = visible_slots(span_ids[0], cache_counts[0], span_mask)

    def cut_queries(other):
        return lax.dynamic_slice(qkv[0, :, 0], (0, other * width), (own_rows, width))

    queries = heads_gathered(cut_queries, own_rows, place, devices)
    far_parts = far_mix(queries, cache_kv, live_slots)

    pairs = width // PAIR
    front = (pairs + 1) // 2
    heads_all = None
    for first, count in ((0, front), (front, pairs - front)):

        def cut_kv(other):
            begin = (0, other * width + first * PAIR)
            size = (own_rows, count * PAIR)
            return jnp.stack([lax.dynamic_slice(qkv[0, :, i], begin, size) for i in (1, 2)])

        own_kv = heads_gathered(cut_kv, own_rows, place, devices)
        heads_all = near_mix(queries, own_kv, far_parts, first, heads_all)

    resid_prev = passed_along(resid[0], "section", 1)
    gate_prev = passed_along(gate[0], "section", 1)
    moved = summed_and_moved(heads_all, out_proj, devices).astype(jnp.float32)
    video_of = (place * own_rows + jnp.arange(own_rows, dtype=jnp.int32)) // SPAN
    gains = jnp.where((video_of == 0)[:, None], gate_prev[0:1], gate_prev[1:2])
    return (resid_prev + gains * moved)[None]


def solution(mesh):
    in_specs = (
        P("section", "sp", None),
        P("section", "sp", None, None),
        P("section", None, None, None, "sp"),
        P("section", "sp", None),
        P("section", None, None),
        P("section"),
        P("section"),
        P(),
    )
    out_specs = P("section", "sp", None)
    return jax.shard_map(
        per_device, mesh=mesh, in_specs=in_specs, out_specs=out_specs, check_vma=False
    )
```

```python
import math

import jax
import jax.numpy as jnp
from jax import lax
from jax.experimental import pallas as pl
from jax.experimental.pallas import tpu as pltpu
from jax.sharding import PartitionSpec as P

HDIM = 128
SPAN = 448
NCHUNK = 40
SLOTS = 3
VIDS = 2
TOKS = 896
KEYS = 1344
PAIR = 2 * HDIM
FLOOR = -3.0e38
SCALE = HDIM ** (-0.5) * math.log2(math.e)
COLS = 256
LAG = 3


def swapped(shard, axis, bit):
    devices = lax.axis_size(axis)
    return lax.ppermute(shard, axis, [(i, i ^ bit) for i in range(devices)])


def passed_along(shard, axis, by):
    devices = lax.axis_size(axis)
    return lax.ppermute(shard, axis, [(i, (i + by) % devices) for i in range(devices)])


def visible_slots(span_id, filled, span_mask):
    row_mask = lax.dynamic_index_in_dim(span_mask, span_id, 0, keepdims=False)
    slot_ids = jnp.arange(SLOTS, dtype=jnp.int32)
    wanted = span_id - 1 - slot_ids
    columns = jnp.arange(NCHUNK, dtype=jnp.int32)
    looked = jnp.sum(jnp.where(columns[None, :] == wanted[:, None], row_mask[None, :], 0), axis=1)
    return (slot_ids < filled) & (looked == 1)


def dot_t(left, right):
    return lax.dot_general(left, right, (((1,), (1,)), ((), ())), preferred_element_type=jnp.float32)


def far_kernel(q_ref, k_ref, v_ref, bias_ref, acc_ref, high_ref, total_ref):
    for head in range(2):
        cols = slice(head * HDIM, (head + 1) * HDIM)
        scores = dot_t(q_ref[:, cols], k_ref[0, 0, 0, :, cols]) + bias_ref[0:1, :]
        highest = jnp.maximum(jnp.max(scores, axis=1, keepdims=True), FLOOR)
        raised = jnp.exp2(scores * SCALE - highest * SCALE)
        total = jnp.sum(raised, axis=1, keepdims=True)
        acc_ref[:, cols] = jnp.dot(
            raised.astype(jnp.bfloat16), v_ref[0, 0, 0, :, cols], preferred_element_type=jnp.float32
        )
        high_ref[:, cols] = jnp.broadcast_to(highest, (SPAN, HDIM))
        total_ref[:, cols] = jnp.broadcast_to(total, (SPAN, HDIM))


def near_kernel(q_ref, k_ref, v_ref, acc_ref, high_ref, total_ref, *rest):
    out_ref = rest[-1]
    for head in range(2):
        cols = slice(head * HDIM, (head + 1) * HDIM)
        scores = dot_t(q_ref[:, cols], k_ref[0, :, cols])
        far_high = high_ref[:, cols]
        near_high = jnp.broadcast_to(jnp.max(scores, axis=1, keepdims=True), (SPAN, HDIM))
        highest = jnp.maximum(near_high, far_high) * SCALE
        wide = jnp.concatenate([highest] * -(-SPAN // HDIM), axis=1)[:, :SPAN]
        raised = jnp.exp2(scores * SCALE - wide)
        fade = jnp.exp2(far_high * SCALE - highest)
        near_total = jnp.broadcast_to(jnp.sum(raised, axis=1, keepdims=True), (SPAN, HDIM))
        total = near_total + total_ref[:, cols] * fade
        mixed = jnp.dot(raised.astype(jnp.bfloat16), v_ref[0, :, cols], preferred_element_type=jnp.float32)
        mixed = (mixed + acc_ref[:, cols] * fade) / total
        out_ref[:, cols] = mixed.astype(jnp.bfloat16)


def far_mix(queries, cache_kv, live_slots):
    width = queries.shape[1]
    bias = jnp.where(jnp.repeat(live_slots, SPAN), 0.0, -jnp.inf).astype(jnp.float32)
    bias = jnp.broadcast_to(bias[None, :], (8, KEYS))
    block = pl.BlockSpec((SPAN, PAIR), lambda b, h: (b, h))
    return pl.pallas_call(
        far_kernel,
        grid=(VIDS, width // PAIR),
        in_specs=[
            block,
            pl.BlockSpec((1, 1, 1, KEYS, PAIR), lambda b, h: (0, 0, b, 0, h)),
            pl.BlockSpec((1, 1, 1, KEYS, PAIR), lambda b, h: (0, 1, b, 0, h)),
            pl.BlockSpec((8, KEYS), lambda b, h: (0, 0)),
        ],
        out_specs=[block] * 3,
        out_shape=[jax.ShapeDtypeStruct((TOKS, width), jnp.float32)] * 3,
        compiler_params=pltpu.CompilerParams(vmem_limit_bytes=40 * 1024 * 1024),
        cost_estimate=pl.CostEstimate(
            flops=4 * TOKS * KEYS * width,
            bytes_accessed=TOKS * width,
            transcendentals=0,
        ),
    )(queries, cache_kv, cache_kv, bias)


def near_mix(queries, own_kv, far_parts, first, earlier):
    width, group = queries.shape[1], own_kv.shape[2]
    block = pl.BlockSpec((SPAN, PAIR), lambda b, h: (b, h + first))
    operands = [queries, own_kv, own_kv, *far_parts]
    in_specs = [
        block,
        pl.BlockSpec((1, SPAN, PAIR), lambda b, h: (0, b, h)),
        pl.BlockSpec((1, SPAN, PAIR), lambda b, h: (1, b, h)),
        block,
        block,
        block,
    ]
    aliases = {}
    if earlier is not None:
        aliases = {len(operands): 0}
        operands.append(earlier)
        in_specs.append(pl.BlockSpec(memory_space=pl.ANY))
    return pl.pallas_call(
        near_kernel,
        grid=(VIDS, group // PAIR),
        in_specs=in_specs,
        out_specs=block,
        out_shape=jax.ShapeDtypeStruct((TOKS, width), jnp.bfloat16),
        input_output_aliases=aliases,
        compiler_params=pltpu.CompilerParams(vmem_limit_bytes=40 * 1024 * 1024),
        cost_estimate=pl.CostEstimate(
            flops=4 * TOKS * SPAN * group,
            bytes_accessed=TOKS * group,
            transcendentals=0,
        ),
    )(*operands)


def flipped(place, bits):
    bit = 1
    while bit <= bits:
        if bits & bit:
            place = place + bit - 2 * bit * lax.rem(lax.div(place, bit), 2)
        bit *= 2
    return place


def sum_kernel(devices, heads_ref, proj_ref, out_ref, w_buf, acc, *rest):
    stages = devices.bit_length() - 1
    sends, lands = rest[: stages + 1], rest[stages + 1 : 2 * stages + 1]
    w_sem, send_sem, recv_sem = rest[2 * stages + 1 :]
    place, section = lax.axis_index("sp"), lax.axis_index("section")
    sections = lax.axis_size("section")
    after = lax.rem(section + 1, sections)
    before = lax.rem(section + sections - 1, sections)
    rows = heads_ref.shape[0] // devices
    chunks = acc.shape[0]
    cols = acc.shape[2]
    mesh_id = pl.DeviceIdType.MESH
    partners = [(section, flipped(place, 1 << k)) for k in range(stages)]

    first_fetch = pltpu.make_async_copy(proj_ref.at[0, :, pl.ds(0, cols)], w_buf.at[0], w_sem.at[0])
    first_fetch.start()
    barrier = pltpu.get_barrier_semaphore()
    for other in partners + [(before, place)]:
        pl.semaphore_signal(barrier, inc=1, device_id=other, device_id_type=mesh_id)
    pl.semaphore_wait(barrier, stages + 1)

    def columns(t):
        return pl.ds(pl.multiple_of(t * cols, cols), cols)

    def fetch(t):
        slot = lax.rem(t, 2)
        return pltpu.make_async_copy(proj_ref.at[0, :, columns(t)], w_buf.at[slot], w_sem.at[slot])

    def move(k, t):
        return pltpu.make_async_remote_copy(
            src_ref=sends[k].at[t],
            dst_ref=lands[k].at[t] if k < stages else out_ref.at[:, columns(t)],
            send_sem=send_sem.at[k, t],
            recv_sem=recv_sem.at[k, t],
            device_id=partners[k] if k < stages else (after, place),
            device_id_type=mesh_id,
        )

    def product(t, flips):
        start = pl.multiple_of(flipped(place, flips) * rows, 16)
        return jnp.dot(
            heads_ref[pl.ds(start, rows), :], w_buf[lax.rem(t, 2)], preferred_element_type=jnp.float32
        )

    def multiply(t):
        fetch(t).wait()

        @pl.when(t + 1 < chunks)
        def _():
            fetch(t + 1).start()

        for i in range(devices // 2):
            sends[0][t, i * rows : (i + 1) * rows] = product(t, 2 * i + 1).astype(jnp.bfloat16)
        move(0, t).start()
        for i in range(devices // 2):
            acc[t, i * rows : (i + 1) * rows] = product(t, 2 * i)

    def combine(k, t):
        move(k, t).wait_recv()
        count = devices >> (k + 1)
        for i in range(count):
            spot = i << k
            summed = acc[t, spot * rows : (spot + 1) * rows] + lands[k][
                t, i * rows : (i + 1) * rows
            ].astype(jnp.float32)
            if i % 2 or count == 1:
                j = i // 2
                sends[k + 1][t, j * rows : (j + 1) * rows] = summed.astype(jnp.bfloat16)
            else:
                acc[t, spot * rows : (spot + 1) * rows] = summed
        move(k + 1, t).start()

    def step(t, carry):
        @pl.when(t < chunks)
        def _():
            multiply(t)

        for k in range(stages):
            done = t - LAG * (k + 1)

            @pl.when((done >= 0) & (done < chunks))
            def _():
                combine(k, done)

        return carry

    lax.fori_loop(0, chunks + LAG * stages, step, 0)

    def finish(t, carry):
        move(stages, t).wait_recv()
        for k in range(stages + 1):
            move(k, t).wait_send()
        return carry

    lax.fori_loop(0, chunks, finish, 0)


def summed_and_moved(heads_all, out_proj, devices):
    width, model = out_proj.shape[1], out_proj.shape[2]
    rows = TOKS // devices
    chunks = model // COLS
    stages = devices.bit_length() - 1
    sizes = [max(devices >> (k + 1), 1) * rows for k in range(stages + 1)]
    return pl.pallas_call(
        lambda *refs: sum_kernel(devices, *refs),
        out_shape=jax.ShapeDtypeStruct((rows, model), jnp.bfloat16),
        in_specs=[pl.BlockSpec(memory_space=pltpu.VMEM), pl.BlockSpec(memory_space=pl.ANY)],
        out_specs=pl.BlockSpec(memory_space=pl.ANY),
        scratch_shapes=[
            pltpu.VMEM((2, width, COLS), jnp.bfloat16),
            pltpu.VMEM((chunks, sizes[0], COLS), jnp.float32),
        ]
        + [pltpu.VMEM((chunks, size, COLS), jnp.bfloat16) for size in sizes]
        + [pltpu.VMEM((chunks, size, COLS), jnp.bfloat16) for size in sizes[:-1]]
        + [
            pltpu.SemaphoreType.DMA((2,)),
            pltpu.SemaphoreType.DMA((stages + 1, chunks)),
            pltpu.SemaphoreType.DMA((stages + 1, chunks)),
        ],
        compiler_params=pltpu.CompilerParams(
            collective_id=0, has_side_effects=True, vmem_limit_bytes=58 * 1024 * 1024
        ),
        cost_estimate=pl.CostEstimate(
            flops=2 * TOKS * width * model, bytes_accessed=2 * width * model, transcendentals=0
        ),
    )(heads_all, out_proj)


def heads_gathered(cut, rows, place, devices):
    piece = cut(place)
    whole = jnp.zeros(piece.shape[:-2] + (rows * devices, piece.shape[-1]), piece.dtype)
    lead = (0,) * (piece.ndim - 2)
    near_piece = piece
    for bit in range(devices):
        other = place ^ bit
        piece = cut(other)
        if bit:
            piece = swapped(piece, "sp", bit)
        if bit == 1:
            near_piece = piece
        whole = lax.dynamic_update_slice(whole, piece, (*lead, other * rows, 0))
    return whole, near_piece


def per_device(resid, qkv, cache_kv, out_proj, gate, span_ids, cache_counts, span_mask):
    own_rows = resid.shape[1]
    width = cache_kv.shape[4]
    devices = lax.axis_size("sp")
    place = lax.axis_index("sp")
    live_slots = visible_slots(span_ids[0], cache_counts[0], span_mask)

    def cut_queries(other):
        return lax.dynamic_slice(qkv[0, :, 0], (0, other * width), (own_rows, width))

    queries, near_piece = heads_gathered(cut_queries, own_rows, place, devices)
    far_parts = far_mix(queries, cache_kv, live_slots)

    pairs = width // PAIR
    front = (pairs + 1) // 2
    heads_all = None
    for first, count, awaited in ((0, front, near_piece), (front, pairs - front, queries)):
        source, _ = lax.optimization_barrier((qkv, awaited))

        def cut_kv(other):
            begin = (0, other * width + first * PAIR)
            size = (own_rows, count * PAIR)
            return jnp.stack([lax.dynamic_slice(source[0, :, i], begin, size) for i in (1, 2)])

        own_kv, _ = heads_gathered(cut_kv, own_rows, place, devices)
        heads_all = near_mix(queries, own_kv, far_parts, first, heads_all)

    resid_prev = passed_along(resid[0], "section", 1)
    gate_prev = passed_along(gate[0], "section", 1)
    moved = summed_and_moved(heads_all, out_proj, devices).astype(jnp.float32)
    video_of = (place * own_rows + jnp.arange(own_rows, dtype=jnp.int32)) // SPAN
    gains = jnp.where((video_of == 0)[:, None], gate_prev[0:1], gate_prev[1:2])
    return (resid_prev + gains * moved)[None]


def solution(mesh):
    in_specs = (
        P("section", "sp", None),
        P("section", "sp", None, None),
        P("section", None, None, None, "sp"),
        P("section", "sp", None),
        P("section", None, None),
        P("section"),
        P("section"),
        P(),
    )
    out_specs = P("section", "sp", None)
    return jax.shard_map(
        per_device, mesh=mesh, in_specs=in_specs, out_specs=out_specs, check_vma=False
    )
```

```python
import math

import jax
import jax.numpy as jnp
from jax import lax
from jax.experimental import pallas as pl
from jax.experimental.pallas import tpu as pltpu
from jax.sharding import PartitionSpec as P

HDIM = 128
SPAN = 448
NCHUNK = 40
SLOTS = 3
VIDS = 2
TOKS = 896
KEYS = 1344
PAIR = 2 * HDIM
FLOOR = -3.0e37
TINY = 1.0e-30
SCALE = HDIM ** (-0.5) * math.log2(math.e)
COLS = 256
LAG = 3


def swapped(shard, axis, bit):
    devices = lax.axis_size(axis)
    return lax.ppermute(shard, axis, [(i, i ^ bit) for i in range(devices)])


def passed_along(shard, axis, by):
    devices = lax.axis_size(axis)
    return lax.ppermute(shard, axis, [(i, (i + by) % devices) for i in range(devices)])


def visible_slots(span_id, filled, span_mask):
    row_mask = lax.dynamic_index_in_dim(span_mask, span_id, 0, keepdims=False)
    slot_ids = jnp.arange(SLOTS, dtype=jnp.int32)
    wanted = span_id - 1 - slot_ids
    columns = jnp.arange(NCHUNK, dtype=jnp.int32)
    looked = jnp.sum(jnp.where(columns[None, :] == wanted[:, None], row_mask[None, :], 0), axis=1)
    return (slot_ids < filled) & (looked == 1)


def dot_t(left, right):
    return lax.dot_general(left, right, (((1,), (1,)), ((), ())), preferred_element_type=jnp.float32)


def lane_of(head):
    return lax.broadcasted_iota(jnp.int32, (SPAN, HDIM), 1) == head


def attend_part(queries, keys, values, bias):
    scores = dot_t(queries, keys)
    if bias is not None:
        scores = scores + bias
    highest = jnp.maximum(jnp.max(scores, axis=1, keepdims=True), FLOOR) * SCALE
    raised = jnp.exp2(scores * SCALE - highest)
    total = jnp.sum(raised, axis=1, keepdims=True)
    mixed = jnp.dot(raised.astype(jnp.bfloat16), values, preferred_element_type=jnp.float32)
    return mixed / jnp.maximum(total, TINY), highest + jnp.log2(total)


def far_kernel(q_ref, k_ref, v_ref, bias_ref, out_ref, level_ref):
    step = pl.program_id(1)

    @pl.when(step == 0)
    def _():
        level_ref[...] = jnp.zeros_like(level_ref)

    for head in range(2):
        cols = slice(head * HDIM, (head + 1) * HDIM)
        mixed, level = attend_part(
            q_ref[:, cols], k_ref[0, 0, 0, :, cols], v_ref[0, 0, 0, :, cols], bias_ref[0:1, :]
        )
        out_ref[:, cols] = mixed
        level_ref[...] = jnp.where(lane_of(2 * step + head), level, level_ref[...])


def near_kernel(q_ref, k_ref, v_ref, out_ref, level_ref):
    step = pl.program_id(0)

    @pl.when(step == 0)
    def _():
        level_ref[...] = jnp.zeros_like(level_ref)

    for head in range(2):
        cols = slice(head * HDIM, (head + 1) * HDIM)
        mixed, level = attend_part(q_ref[:, cols], k_ref[0, :, cols], v_ref[0, :, cols], None)
        out_ref[:, cols] = mixed.astype(jnp.bfloat16)
        level_ref[...] = jnp.where(lane_of(2 * step + head), level, level_ref[...])


def join_kernel(far_ref, far_level_ref, near_ref, near_level_ref, out_ref):
    step = pl.program_id(1)
    share = 1.0 / (1.0 + jnp.exp2(far_level_ref[...] - near_level_ref[...]))
    for head in range(2):
        cols = slice(head * HDIM, (head + 1) * HDIM)
        part = jnp.sum(jnp.where(lane_of(2 * step + head), share, 0.0), axis=1, keepdims=True)
        far = far_ref[:, cols]
        out_ref[:, cols] = (far + (near_ref[:, cols].astype(jnp.float32) - far) * part).astype(jnp.bfloat16)


def far_mix(queries, cache_kv, live_slots):
    width = queries.shape[1]
    bias = jnp.where(jnp.repeat(live_slots, SPAN), 0.0, -jnp.inf).astype(jnp.float32)
    bias = jnp.broadcast_to(bias[None, :], (8, KEYS))
    block = pl.BlockSpec((SPAN, PAIR), lambda b, h: (b, h))
    return pl.pallas_call(
        far_kernel,
        grid=(VIDS, width // PAIR),
        in_specs=[
            block,
            pl.BlockSpec((1, 1, 1, KEYS, PAIR), lambda b, h: (0, 0, b, 0, h)),
            pl.BlockSpec((1, 1, 1, KEYS, PAIR), lambda b, h: (0, 1, b, 0, h)),
            pl.BlockSpec((8, KEYS), lambda b, h: (0, 0)),
        ],
        out_specs=[block, pl.BlockSpec((SPAN, HDIM), lambda b, h: (b, 0))],
        out_shape=[
            jax.ShapeDtypeStruct((TOKS, width), jnp.float32),
            jax.ShapeDtypeStruct((TOKS, HDIM), jnp.float32),
        ],
        compiler_params=pltpu.CompilerParams(vmem_limit_bytes=40 * 1024 * 1024),
        cost_estimate=pl.CostEstimate(
            flops=4 * TOKS * KEYS * width, bytes_accessed=TOKS * width, transcendentals=0
        ),
    )(queries, cache_kv, cache_kv, bias)


def near_mix(queries, own_kv):
    width = queries.shape[1]
    block = pl.BlockSpec((SPAN, PAIR), lambda h: (0, h))
    return pl.pallas_call(
        near_kernel,
        grid=(width // PAIR,),
        in_specs=[
            block,
            pl.BlockSpec((1, SPAN, PAIR), lambda h: (0, 0, h)),
            pl.BlockSpec((1, SPAN, PAIR), lambda h: (1, 0, h)),
        ],
        out_specs=[block, pl.BlockSpec((SPAN, HDIM), lambda h: (0, 0))],
        out_shape=[
            jax.ShapeDtypeStruct((SPAN, width), jnp.bfloat16),
            jax.ShapeDtypeStruct((SPAN, HDIM), jnp.float32),
        ],
        compiler_params=pltpu.CompilerParams(vmem_limit_bytes=40 * 1024 * 1024),
        cost_estimate=pl.CostEstimate(
            flops=4 * SPAN * SPAN * width, bytes_accessed=SPAN * width, transcendentals=0
        ),
    )(queries, own_kv, own_kv)


def join(far, far_level, near, near_level):
    width = far.shape[1]
    block = pl.BlockSpec((SPAN, PAIR), lambda b, h: (b, h))
    level = pl.BlockSpec((SPAN, HDIM), lambda b, h: (b, 0))
    return pl.pallas_call(
        join_kernel,
        grid=(VIDS, width // PAIR),
        in_specs=[block, level, block, level],
        out_specs=block,
        out_shape=jax.ShapeDtypeStruct((TOKS, width), jnp.bfloat16),
        compiler_params=pltpu.CompilerParams(vmem_limit_bytes=40 * 1024 * 1024),
        cost_estimate=pl.CostEstimate(
            flops=TOKS * width, bytes_accessed=TOKS * width, transcendentals=0
        ),
    )(far, far_level, near, near_level)


def flipped(place, bits):
    bit = 1
    while bit <= bits:
        if bits & bit:
            place = place + bit - 2 * bit * lax.rem(lax.div(place, bit), 2)
        bit *= 2
    return place


def sum_kernel(devices, heads_ref, proj_ref, out_ref, w_buf, acc, *rest):
    stages = devices.bit_length() - 1
    sends, lands = rest[: stages + 1], rest[stages + 1 : 2 * stages + 1]
    w_sem, send_sem, recv_sem = rest[2 * stages + 1 :]
    place, section = lax.axis_index("sp"), lax.axis_index("section")
    sections = lax.axis_size("section")
    after = lax.rem(section + 1, sections)
    before = lax.rem(section + sections - 1, sections)
    rows = heads_ref.shape[0] // devices
    chunks = acc.shape[0]
    cols = acc.shape[2]
    mesh_id = pl.DeviceIdType.MESH
    partners = [(section, flipped(place, 1 << k)) for k in range(stages)]

    first_fetch = pltpu.make_async_copy(proj_ref.at[0, :, pl.ds(0, cols)], w_buf.at[0], w_sem.at[0])
    first_fetch.start()
    barrier = pltpu.get_barrier_semaphore()
    for other in partners + [(before, place)]:
        pl.semaphore_signal(barrier, inc=1, device_id=other, device_id_type=mesh_id)
    pl.semaphore_wait(barrier, stages + 1)

    def columns(t):
        return pl.ds(pl.multiple_of(t * cols, cols), cols)

    def fetch(t):
        slot = lax.rem(t, 2)
        return pltpu.make_async_copy(proj_ref.at[0, :, columns(t)], w_buf.at[slot], w_sem.at[slot])

    def move(k, t):
        return pltpu.make_async_remote_copy(
            src_ref=sends[k].at[t],
            dst_ref=lands[k].at[t] if k < stages else out_ref.at[:, columns(t)],
            send_sem=send_sem.at[k, t],
            recv_sem=recv_sem.at[k, t],
            device_id=partners[k] if k < stages else (after, place),
            device_id_type=mesh_id,
        )

    def product(t, flips):
        start = pl.multiple_of(flipped(place, flips) * rows, 16)
        return jnp.dot(
            heads_ref[pl.ds(start, rows), :], w_buf[lax.rem(t, 2)], preferred_element_type=jnp.float32
        )

    def multiply(t):
        fetch(t).wait()

        @pl.when(t + 1 < chunks)
        def _():
            fetch(t + 1).start()

        for i in range(devices // 2):
            sends[0][t, i * rows : (i + 1) * rows] = product(t, 2 * i + 1).astype(jnp.bfloat16)
        move(0, t).start()
        for i in range(devices // 2):
            acc[t, i * rows : (i + 1) * rows] = product(t, 2 * i)

    def combine(k, t):
        move(k, t).wait_recv()
        count = devices >> (k + 1)
        for i in range(count):
            spot = i << k
            summed = acc[t, spot * rows : (spot + 1) * rows] + lands[k][
                t, i * rows : (i + 1) * rows
            ].astype(jnp.float32)
            if i % 2 or count == 1:
                j = i // 2
                sends[k + 1][t, j * rows : (j + 1) * rows] = summed.astype(jnp.bfloat16)
            else:
                acc[t, spot * rows : (spot + 1) * rows] = summed
        move(k + 1, t).start()

    def step(t, carry):
        @pl.when(t < chunks)
        def _():
            multiply(t)

        for k in range(stages):
            done = t - LAG * (k + 1)

            @pl.when((done >= 0) & (done < chunks))
            def _():
                combine(k, done)

        return carry

    lax.fori_loop(0, chunks + LAG * stages, step, 0)

    def finish(t, carry):
        move(stages, t).wait_recv()
        for k in range(stages + 1):
            move(k, t).wait_send()
        return carry

    lax.fori_loop(0, chunks, finish, 0)


def summed_and_moved(heads_all, out_proj, devices):
    width, model = out_proj.shape[1], out_proj.shape[2]
    rows = TOKS // devices
    chunks = model // COLS
    stages = devices.bit_length() - 1
    sizes = [max(devices >> (k + 1), 1) * rows for k in range(stages + 1)]
    return pl.pallas_call(
        lambda *refs: sum_kernel(devices, *refs),
        out_shape=jax.ShapeDtypeStruct((rows, model), jnp.bfloat16),
        in_specs=[pl.BlockSpec(memory_space=pltpu.VMEM), pl.BlockSpec(memory_space=pl.ANY)],
        out_specs=pl.BlockSpec(memory_space=pl.ANY),
        scratch_shapes=[
            pltpu.VMEM((2, width, COLS), jnp.bfloat16),
            pltpu.VMEM((chunks, sizes[0], COLS), jnp.float32),
        ]
        + [pltpu.VMEM((chunks, size, COLS), jnp.bfloat16) for size in sizes]
        + [pltpu.VMEM((chunks, size, COLS), jnp.bfloat16) for size in sizes[:-1]]
        + [
            pltpu.SemaphoreType.DMA((2,)),
            pltpu.SemaphoreType.DMA((stages + 1, chunks)),
            pltpu.SemaphoreType.DMA((stages + 1, chunks)),
        ],
        compiler_params=pltpu.CompilerParams(
            collective_id=0, has_side_effects=True, vmem_limit_bytes=58 * 1024 * 1024
        ),
        cost_estimate=pl.CostEstimate(
            flops=2 * TOKS * width * model, bytes_accessed=2 * width * model, transcendentals=0
        ),
    )(heads_all, out_proj)


def rows_gathered(cut, rows, place, group):
    piece = cut(place)
    whole = jnp.zeros(piece.shape[:-2] + (rows * group, piece.shape[-1]), piece.dtype)
    lead = (0,) * (piece.ndim - 2)
    for bit in range(group):
        other = place ^ bit
        piece = cut(other)
        if bit:
            piece = swapped(piece, "sp", bit)
        whole = lax.dynamic_update_slice(whole, piece, (*lead, other % group * rows, 0))
    return whole


def both_videos(own, other, video):
    whole = jnp.zeros((TOKS, own.shape[1]), own.dtype)
    whole = lax.dynamic_update_slice(whole, own, (video * SPAN, 0))
    return lax.dynamic_update_slice(whole, other, ((1 - video) * SPAN, 0))


def per_device(resid, qkv, cache_kv, out_proj, gate, span_ids, cache_counts, span_mask):
    own_rows = resid.shape[1]
    width = cache_kv.shape[4]
    heads = width // HDIM
    devices = lax.axis_size("sp")
    group = devices // VIDS
    place = lax.axis_index("sp")
    video = place // group
    live_slots = visible_slots(span_ids[0], cache_counts[0], span_mask)

    def gathered(across, parts, source):
        def cut(other):
            holder = other ^ group if across else other
            begin, size = (0, holder * width), (own_rows, width)
            cuts = [lax.dynamic_slice(source[0, :, i], begin, size) for i in parts]
            return cuts[0] if len(cuts) == 1 else jnp.stack(cuts)

        return rows_gathered(cut, own_rows, place, group)

    across_q = gathered(True, (0,), qkv)
    other_q = swapped(across_q, "sp", group)
    source, _ = lax.optimization_barrier((qkv, across_q))
    across_kv = gathered(True, (1, 2), source)
    source, _ = lax.optimization_barrier((qkv, across_kv))
    own_q = gathered(False, (0,), source)
    own_kv = gathered(False, (1, 2), source)

    across_out, across_level = near_mix(across_q, across_kv)
    other_out = swapped(across_out, "sp", group)
    other_level = swapped(across_level[:, :heads].T, "sp", group).T
    other_level = jnp.pad(other_level, ((0, 0), (0, HDIM - heads)))

    queries = both_videos(own_q, other_q, video)
    queries, _ = lax.optimization_barrier((queries, across_out))
    far, far_level = far_mix(queries, cache_kv, live_slots)
    own_out, own_level = near_mix(own_q, own_kv)
    near = both_videos(own_out, other_out, video)
    near_level = both_videos(own_level, other_level, video)
    heads_all = join(far, far_level, near, near_level)

    resid_prev = passed_along(resid[0], "section", 1)
    gate_prev = passed_along(gate[0], "section", 1)
    moved = summed_and_moved(heads_all, out_proj, devices).astype(jnp.float32)
    video_of = (place * own_rows + jnp.arange(own_rows, dtype=jnp.int32)) // SPAN
    gains = jnp.where((video_of == 0)[:, None], gate_prev[0:1], gate_prev[1:2])
    return (resid_prev + gains * moved)[None]


def solution(mesh):
    in_specs = (
        P("section", "sp", None),
        P("section", "sp", None, None),
        P("section", None, None, None, "sp"),
        P("section", "sp", None),
        P("section", None, None),
        P("section"),
        P("section"),
        P(),
    )
    out_specs = P("section", "sp", None)
    return jax.shard_map(
        per_device, mesh=mesh, in_specs=in_specs, out_specs=out_specs, check_vma=False
    )
```

```python
import math

import jax
import jax.numpy as jnp
from jax import lax
from jax.experimental import pallas as pl
from jax.experimental.pallas import tpu as pltpu
from jax.sharding import PartitionSpec as P

HDIM = 128
SPAN = 448
NCHUNK = 40
SLOTS = 3
VIDS = 2
TOKS = 896
KEYS = 1344
PAIR = 2 * HDIM
FLOOR = -3.0e37
TINY = 1.0e-30
SCALE = HDIM ** (-0.5) * math.log2(math.e)
COLS = 256
LAG = 3


def swapped(shard, axis, bit):
    devices = lax.axis_size(axis)
    return lax.ppermute(shard, axis, [(i, i ^ bit) for i in range(devices)])


def passed_along(shard, axis, by):
    devices = lax.axis_size(axis)
    return lax.ppermute(shard, axis, [(i, (i + by) % devices) for i in range(devices)])


def visible_slots(span_id, filled, span_mask):
    row_mask = lax.dynamic_index_in_dim(span_mask, span_id, 0, keepdims=False)
    slot_ids = jnp.arange(SLOTS, dtype=jnp.int32)
    wanted = span_id - 1 - slot_ids
    columns = jnp.arange(NCHUNK, dtype=jnp.int32)
    looked = jnp.sum(jnp.where(columns[None, :] == wanted[:, None], row_mask[None, :], 0), axis=1)
    return (slot_ids < filled) & (looked == 1)


def dot_t(left, right):
    return lax.dot_general(left, right, (((1,), (1,)), ((), ())), preferred_element_type=jnp.float32)


def lane_of(head):
    return lax.broadcasted_iota(jnp.int32, (SPAN, HDIM), 1) == head


def attend_part(queries, keys, values, bias):
    scores = dot_t(queries, keys)
    if bias is not None:
        scores = scores + bias
    highest = jnp.maximum(jnp.max(scores, axis=1, keepdims=True), FLOOR) * SCALE
    raised = jnp.exp2(scores * SCALE - highest)
    total = jnp.sum(raised, axis=1, keepdims=True)
    mixed = jnp.dot(raised.astype(jnp.bfloat16), values, preferred_element_type=jnp.float32)
    return mixed / jnp.maximum(total, TINY), highest + jnp.log2(total)


def far_kernel(q_ref, k_ref, v_ref, bias_ref, out_ref, level_ref):
    step = pl.program_id(1)

    @pl.when(step == 0)
    def _():
        level_ref[...] = jnp.zeros_like(level_ref)

    for head in range(2):
        cols = slice(head * HDIM, (head + 1) * HDIM)
        mixed, level = attend_part(
            q_ref[:, cols], k_ref[0, 0, 0, :, cols], v_ref[0, 0, 0, :, cols], bias_ref[0:1, :]
        )
        out_ref[:, cols] = mixed
        level_ref[...] = jnp.where(lane_of(2 * step + head), level, level_ref[...])


def near_kernel(q_ref, k_ref, v_ref, out_ref, level_ref):
    step = pl.program_id(0)

    @pl.when(step == 0)
    def _():
        level_ref[...] = jnp.zeros_like(level_ref)

    for head in range(2):
        cols = slice(head * HDIM, (head + 1) * HDIM)
        mixed, level = attend_part(q_ref[:, cols], k_ref[0, :, cols], v_ref[0, :, cols], None)
        out_ref[:, cols] = mixed.astype(jnp.bfloat16)
        level_ref[...] = jnp.where(lane_of(2 * step + head), level, level_ref[...])


def join_kernel(far_ref, far_level_ref, near_ref, near_level_ref, out_ref):
    step = pl.program_id(1)
    share = 1.0 / (1.0 + jnp.exp2(far_level_ref[...] - near_level_ref[...]))
    for head in range(2):
        cols = slice(head * HDIM, (head + 1) * HDIM)
        part = jnp.sum(jnp.where(lane_of(2 * step + head), share, 0.0), axis=1, keepdims=True)
        far = far_ref[:, cols]
        out_ref[:, cols] = (far + (near_ref[:, cols].astype(jnp.float32) - far) * part).astype(jnp.bfloat16)


def far_mix(queries, cache_kv, live_slots):
    width = queries.shape[1]
    bias = jnp.where(jnp.repeat(live_slots, SPAN), 0.0, -jnp.inf).astype(jnp.float32)
    bias = jnp.broadcast_to(bias[None, :], (8, KEYS))
    block = pl.BlockSpec((SPAN, PAIR), lambda b, h: (b, h))
    return pl.pallas_call(
        far_kernel,
        grid=(VIDS, width // PAIR),
        in_specs=[
            block,
            pl.BlockSpec((1, 1, 1, KEYS, PAIR), lambda b, h: (0, 0, b, 0, h)),
            pl.BlockSpec((1, 1, 1, KEYS, PAIR), lambda b, h: (0, 1, b, 0, h)),
            pl.BlockSpec((8, KEYS), lambda b, h: (0, 0)),
        ],
        out_specs=[block, pl.BlockSpec((SPAN, HDIM), lambda b, h: (b, 0))],
        out_shape=[
            jax.ShapeDtypeStruct((TOKS, width), jnp.float32),
            jax.ShapeDtypeStruct((TOKS, HDIM), jnp.float32),
        ],
        compiler_params=pltpu.CompilerParams(vmem_limit_bytes=40 * 1024 * 1024),
        cost_estimate=pl.CostEstimate(
            flops=4 * TOKS * KEYS * width, bytes_accessed=TOKS * width, transcendentals=0
        ),
    )(queries, cache_kv, cache_kv, bias)


def near_mix(queries, own_kv):
    width = queries.shape[1]
    block = pl.BlockSpec((SPAN, PAIR), lambda h: (0, h))
    return pl.pallas_call(
        near_kernel,
        grid=(width // PAIR,),
        in_specs=[
            block,
            pl.BlockSpec((1, SPAN, PAIR), lambda h: (0, 0, h)),
            pl.BlockSpec((1, SPAN, PAIR), lambda h: (1, 0, h)),
        ],
        out_specs=[block, pl.BlockSpec((SPAN, HDIM), lambda h: (0, 0))],
        out_shape=[
            jax.ShapeDtypeStruct((SPAN, width), jnp.bfloat16),
            jax.ShapeDtypeStruct((SPAN, HDIM), jnp.float32),
        ],
        compiler_params=pltpu.CompilerParams(vmem_limit_bytes=40 * 1024 * 1024),
        cost_estimate=pl.CostEstimate(
            flops=4 * SPAN * SPAN * width, bytes_accessed=SPAN * width, transcendentals=0
        ),
    )(queries, own_kv, own_kv)


def join(far, far_level, near, near_level):
    width = far.shape[1]
    block = pl.BlockSpec((SPAN, PAIR), lambda b, h: (b, h))
    level = pl.BlockSpec((SPAN, HDIM), lambda b, h: (b, 0))
    return pl.pallas_call(
        join_kernel,
        grid=(VIDS, width // PAIR),
        in_specs=[block, level, block, level],
        out_specs=block,
        out_shape=jax.ShapeDtypeStruct((TOKS, width), jnp.bfloat16),
        compiler_params=pltpu.CompilerParams(vmem_limit_bytes=40 * 1024 * 1024),
        cost_estimate=pl.CostEstimate(
            flops=TOKS * width, bytes_accessed=TOKS * width, transcendentals=0
        ),
    )(far, far_level, near, near_level)


def flipped(place, bits):
    bit = 1
    while bit <= bits:
        if bits & bit:
            place = place + bit - 2 * bit * lax.rem(lax.div(place, bit), 2)
        bit *= 2
    return place


def sum_kernel(devices, heads_ref, proj_ref, out_ref, w_buf, acc, *rest):
    stages = devices.bit_length() - 1
    sends, lands = rest[: stages + 1], rest[stages + 1 : 2 * stages + 1]
    w_sem, send_sem, recv_sem = rest[2 * stages + 1 :]
    place, section = lax.axis_index("sp"), lax.axis_index("section")
    sections = lax.axis_size("section")
    after = lax.rem(section + 1, sections)
    before = lax.rem(section + sections - 1, sections)
    rows = heads_ref.shape[0] // devices
    chunks = acc.shape[0]
    cols = acc.shape[2]
    mesh_id = pl.DeviceIdType.MESH
    partners = [(section, flipped(place, 1 << k)) for k in range(stages)]

    first_fetch = pltpu.make_async_copy(proj_ref.at[0, :, pl.ds(0, cols)], w_buf.at[0], w_sem.at[0])
    first_fetch.start()
    barrier = pltpu.get_barrier_semaphore()
    for other in partners + [(before, place)]:
        pl.semaphore_signal(barrier, inc=1, device_id=other, device_id_type=mesh_id)
    pl.semaphore_wait(barrier, stages + 1)

    def columns(t):
        return pl.ds(pl.multiple_of(t * cols, cols), cols)

    def fetch(t):
        slot = lax.rem(t, 2)
        return pltpu.make_async_copy(proj_ref.at[0, :, columns(t)], w_buf.at[slot], w_sem.at[slot])

    def move(k, t):
        return pltpu.make_async_remote_copy(
            src_ref=sends[k].at[t],
            dst_ref=lands[k].at[t] if k < stages else out_ref.at[:, columns(t)],
            send_sem=send_sem.at[k, t],
            recv_sem=recv_sem.at[k, t],
            device_id=partners[k] if k < stages else (after, place),
            device_id_type=mesh_id,
        )

    def product(t, flips):
        start = pl.multiple_of(flipped(place, flips) * rows, 16)
        return jnp.dot(
            heads_ref[pl.ds(start, rows), :], w_buf[lax.rem(t, 2)], preferred_element_type=jnp.float32
        )

    def multiply(t):
        fetch(t).wait()

        @pl.when(t + 1 < chunks)
        def _():
            fetch(t + 1).start()

        for i in range(devices // 2):
            sends[0][t, i * rows : (i + 1) * rows] = product(t, 2 * i + 1).astype(jnp.bfloat16)
        move(0, t).start()
        for i in range(devices // 2):
            acc[t, i * rows : (i + 1) * rows] = product(t, 2 * i)

    def combine(k, t):
        move(k, t).wait_recv()
        count = devices >> (k + 1)
        for i in range(count):
            spot = i << k
            summed = acc[t, spot * rows : (spot + 1) * rows] + lands[k][
                t, i * rows : (i + 1) * rows
            ].astype(jnp.float32)
            if i % 2 or count == 1:
                j = i // 2
                sends[k + 1][t, j * rows : (j + 1) * rows] = summed.astype(jnp.bfloat16)
            else:
                acc[t, spot * rows : (spot + 1) * rows] = summed
        move(k + 1, t).start()

    def step(t, carry):
        @pl.when(t < chunks)
        def _():
            multiply(t)

        for k in range(stages):
            done = t - LAG * (k + 1)

            @pl.when((done >= 0) & (done < chunks))
            def _():
                combine(k, done)

        return carry

    lax.fori_loop(0, chunks + LAG * stages, step, 0)

    def finish(t, carry):
        move(stages, t).wait_recv()
        for k in range(stages + 1):
            move(k, t).wait_send()
        return carry

    lax.fori_loop(0, chunks, finish, 0)


def summed_and_moved(heads_all, out_proj, devices):
    width, model = out_proj.shape[1], out_proj.shape[2]
    rows = TOKS // devices
    chunks = model // COLS
    stages = devices.bit_length() - 1
    sizes = [max(devices >> (k + 1), 1) * rows for k in range(stages + 1)]
    return pl.pallas_call(
        lambda *refs: sum_kernel(devices, *refs),
        out_shape=jax.ShapeDtypeStruct((rows, model), jnp.bfloat16),
        in_specs=[pl.BlockSpec(memory_space=pltpu.VMEM), pl.BlockSpec(memory_space=pl.ANY)],
        out_specs=pl.BlockSpec(memory_space=pl.ANY),
        scratch_shapes=[
            pltpu.VMEM((2, width, COLS), jnp.bfloat16),
            pltpu.VMEM((chunks, sizes[0], COLS), jnp.float32),
        ]
        + [pltpu.VMEM((chunks, size, COLS), jnp.bfloat16) for size in sizes]
        + [pltpu.VMEM((chunks, size, COLS), jnp.bfloat16) for size in sizes[:-1]]
        + [
            pltpu.SemaphoreType.DMA((2,)),
            pltpu.SemaphoreType.DMA((stages + 1, chunks)),
            pltpu.SemaphoreType.DMA((stages + 1, chunks)),
        ],
        compiler_params=pltpu.CompilerParams(
            collective_id=0, has_side_effects=True, vmem_limit_bytes=58 * 1024 * 1024
        ),
        cost_estimate=pl.CostEstimate(
            flops=2 * TOKS * width * model, bytes_accessed=2 * width * model, transcendentals=0
        ),
    )(heads_all, out_proj)


def rows_gathered(cut, rows, place, group):
    piece = cut(place)
    whole = jnp.zeros(piece.shape[:-2] + (rows * group, piece.shape[-1]), piece.dtype)
    lead = (0,) * (piece.ndim - 2)
    for bit in range(group):
        other = place ^ bit
        piece = cut(other)
        if bit:
            piece = swapped(piece, "sp", bit)
        whole = lax.dynamic_update_slice(whole, piece, (*lead, other % group * rows, 0))
    return whole


def both_videos(own, other, video):
    whole = jnp.zeros((TOKS, own.shape[1]), own.dtype)
    whole = lax.dynamic_update_slice(whole, own, (video * SPAN, 0))
    return lax.dynamic_update_slice(whole, other, ((1 - video) * SPAN, 0))


def per_device(resid, qkv, cache_kv, out_proj, gate, span_ids, cache_counts, span_mask):
    own_rows = resid.shape[1]
    width = cache_kv.shape[4]
    heads = width // HDIM
    devices = lax.axis_size("sp")
    group = devices // VIDS
    place = lax.axis_index("sp")
    video = place // group
    live_slots = visible_slots(span_ids[0], cache_counts[0], span_mask)

    def gathered(across, parts, source):
        def cut(other):
            holder = other ^ group if across else other
            begin, size = (0, holder * width), (own_rows, width)
            cuts = [lax.dynamic_slice(source[0, :, i], begin, size) for i in parts]
            return cuts[0] if len(cuts) == 1 else jnp.stack(cuts)

        return rows_gathered(cut, own_rows, place, group)

    across_q = gathered(True, (0,), qkv)
    other_q = swapped(across_q, "sp", group)
    source, _ = lax.optimization_barrier((qkv, across_q))
    across_kv = gathered(True, (1, 2), source)
    source, _ = lax.optimization_barrier((qkv, across_kv))
    own_q = gathered(False, (0,), source)
    own_kv = gathered(False, (1, 2), source)

    across_out, across_level = near_mix(across_q, across_kv)
    other_out = swapped(across_out, "sp", group)
    other_level = swapped(across_level[:, :heads].T, "sp", group).T
    other_level = jnp.pad(other_level, ((0, 0), (0, HDIM - heads)))

    queries = both_videos(own_q, other_q, video)
    queries, _ = lax.optimization_barrier((queries, across_out))
    far, far_level = far_mix(queries, cache_kv, live_slots)
    own_out, own_level = near_mix(own_q, own_kv)
    near = both_videos(own_out, other_out, video)
    near_level = both_videos(own_level, other_level, video)
    heads_all = join(far, far_level, near, near_level)

    resid_late, gate_late, _ = lax.optimization_barrier((resid, gate, heads_all))
    resid_prev = passed_along(resid_late[0], "section", 1)
    gate_prev = passed_along(gate_late[0], "section", 1)
    moved = summed_and_moved(heads_all, out_proj, devices).astype(jnp.float32)
    video_of = (place * own_rows + jnp.arange(own_rows, dtype=jnp.int32)) // SPAN
    gains = jnp.where((video_of == 0)[:, None], gate_prev[0:1], gate_prev[1:2])
    return (resid_prev + gains * moved)[None]


def solution(mesh):
    in_specs = (
        P("section", "sp", None),
        P("section", "sp", None, None),
        P("section", None, None, None, "sp"),
        P("section", "sp", None),
        P("section", None, None),
        P("section"),
        P("section"),
        P(),
    )
    out_specs = P("section", "sp", None)
    return jax.shard_map(
        per_device, mesh=mesh, in_specs=in_specs, out_specs=out_specs, check_vma=False
    )
```

```python
import math

import jax
import jax.numpy as jnp
from jax import lax
from jax.experimental import pallas as pl
from jax.experimental.pallas import tpu as pltpu
from jax.sharding import PartitionSpec as P

HDIM = 128
SPAN = 448
NCHUNK = 40
SLOTS = 3
VIDS = 2
TOKS = 896
KEYS = 1344
PAIR = 2 * HDIM
FLOOR = -3.0e37
TINY = 1.0e-30
SCALE = HDIM ** (-0.5) * math.log2(math.e)
COLS = 256
LAG = 3


def swapped(shard, axis, bit):
    devices = lax.axis_size(axis)
    return lax.ppermute(shard, axis, [(i, i ^ bit) for i in range(devices)])


def passed_along(shard, axis, by):
    devices = lax.axis_size(axis)
    return lax.ppermute(shard, axis, [(i, (i + by) % devices) for i in range(devices)])


def visible_slots(span_id, filled, span_mask):
    row_mask = lax.dynamic_index_in_dim(span_mask, span_id, 0, keepdims=False)
    slot_ids = jnp.arange(SLOTS, dtype=jnp.int32)
    wanted = span_id - 1 - slot_ids
    columns = jnp.arange(NCHUNK, dtype=jnp.int32)
    looked = jnp.sum(jnp.where(columns[None, :] == wanted[:, None], row_mask[None, :], 0), axis=1)
    return (slot_ids < filled) & (looked == 1)


def dot_t(left, right):
    return lax.dot_general(left, right, (((1,), (1,)), ((), ())), preferred_element_type=jnp.float32)


def lane_of(head):
    return lax.broadcasted_iota(jnp.int32, (SPAN, HDIM), 1) == head


def attend_part(queries, keys, values, bias):
    scores = dot_t(queries, keys)
    if bias is not None:
        scores = scores + bias
    highest = jnp.maximum(jnp.max(scores, axis=1, keepdims=True), FLOOR) * SCALE
    raised = jnp.exp2(scores * SCALE - highest)
    total = jnp.sum(raised, axis=1, keepdims=True)
    mixed = jnp.dot(raised.astype(jnp.bfloat16), values, preferred_element_type=jnp.float32)
    return mixed / jnp.maximum(total, TINY), highest + jnp.log2(total)


def far_kernel(q_ref, k_ref, v_ref, bias_ref, out_ref, level_ref):
    step = pl.program_id(1)

    @pl.when(step == 0)
    def _():
        level_ref[...] = jnp.zeros_like(level_ref)

    for head in range(2):
        cols = slice(head * HDIM, (head + 1) * HDIM)
        mixed, level = attend_part(
            q_ref[:, cols], k_ref[0, 0, 0, :, cols], v_ref[0, 0, 0, :, cols], bias_ref[0:1, :]
        )
        out_ref[:, cols] = mixed
        level_ref[...] = jnp.where(lane_of(2 * step + head), level, level_ref[...])


def near_kernel(q_ref, k_ref, v_ref, out_ref, level_ref):
    step = pl.program_id(0)

    @pl.when(step == 0)
    def _():
        level_ref[...] = jnp.zeros_like(level_ref)

    for head in range(2):
        cols = slice(head * HDIM, (head + 1) * HDIM)
        mixed, level = attend_part(q_ref[:, cols], k_ref[0, :, cols], v_ref[0, :, cols], None)
        out_ref[:, cols] = mixed.astype(jnp.bfloat16)
        level_ref[...] = jnp.where(lane_of(2 * step + head), level, level_ref[...])


def join_kernel(far_ref, far_level_ref, near_ref, near_level_ref, out_ref):
    step = pl.program_id(1)
    share = 1.0 / (1.0 + jnp.exp2(far_level_ref[...] - near_level_ref[...]))
    for head in range(2):
        cols = slice(head * HDIM, (head + 1) * HDIM)
        part = jnp.sum(jnp.where(lane_of(2 * step + head), share, 0.0), axis=1, keepdims=True)
        far = far_ref[:, cols]
        out_ref[:, cols] = (far + (near_ref[:, cols].astype(jnp.float32) - far) * part).astype(jnp.bfloat16)


def far_mix(queries, cache_kv, live_slots):
    width = queries.shape[1]
    bias = jnp.where(jnp.repeat(live_slots, SPAN), 0.0, -jnp.inf).astype(jnp.float32)
    bias = jnp.broadcast_to(bias[None, :], (8, KEYS))
    block = pl.BlockSpec((SPAN, PAIR), lambda b, h: (b, h))
    return pl.pallas_call(
        far_kernel,
        grid=(VIDS, width // PAIR),
        in_specs=[
            block,
            pl.BlockSpec((1, 1, 1, KEYS, PAIR), lambda b, h: (0, 0, b, 0, h)),
            pl.BlockSpec((1, 1, 1, KEYS, PAIR), lambda b, h: (0, 1, b, 0, h)),
            pl.BlockSpec((8, KEYS), lambda b, h: (0, 0)),
        ],
        out_specs=[block, pl.BlockSpec((SPAN, HDIM), lambda b, h: (b, 0))],
        out_shape=[
            jax.ShapeDtypeStruct((TOKS, width), jnp.float32),
            jax.ShapeDtypeStruct((TOKS, HDIM), jnp.float32),
        ],
        compiler_params=pltpu.CompilerParams(vmem_limit_bytes=40 * 1024 * 1024),
        cost_estimate=pl.CostEstimate(
            flops=4 * TOKS * KEYS * width, bytes_accessed=TOKS * width, transcendentals=0
        ),
    )(queries, cache_kv, cache_kv, bias)


def near_mix(queries, own_kv):
    width = queries.shape[1]
    block = pl.BlockSpec((SPAN, PAIR), lambda h: (0, h))
    return pl.pallas_call(
        near_kernel,
        grid=(width // PAIR,),
        in_specs=[
            block,
            pl.BlockSpec((1, SPAN, PAIR), lambda h: (0, 0, h)),
            pl.BlockSpec((1, SPAN, PAIR), lambda h: (1, 0, h)),
        ],
        out_specs=[block, pl.BlockSpec((SPAN, HDIM), lambda h: (0, 0))],
        out_shape=[
            jax.ShapeDtypeStruct((SPAN, width), jnp.bfloat16),
            jax.ShapeDtypeStruct((SPAN, HDIM), jnp.float32),
        ],
        compiler_params=pltpu.CompilerParams(vmem_limit_bytes=40 * 1024 * 1024),
        cost_estimate=pl.CostEstimate(
            flops=4 * SPAN * SPAN * width, bytes_accessed=SPAN * width, transcendentals=0
        ),
    )(queries, own_kv, own_kv)


def join(far, far_level, near, near_level):
    width = far.shape[1]
    block = pl.BlockSpec((SPAN, PAIR), lambda b, h: (b, h))
    level = pl.BlockSpec((SPAN, HDIM), lambda b, h: (b, 0))
    return pl.pallas_call(
        join_kernel,
        grid=(VIDS, width // PAIR),
        in_specs=[block, level, block, level],
        out_specs=block,
        out_shape=jax.ShapeDtypeStruct((TOKS, width), jnp.bfloat16),
        compiler_params=pltpu.CompilerParams(vmem_limit_bytes=40 * 1024 * 1024),
        cost_estimate=pl.CostEstimate(
            flops=TOKS * width, bytes_accessed=TOKS * width, transcendentals=0
        ),
    )(far, far_level, near, near_level)


def flipped(place, bits):
    bit = 1
    while bit <= bits:
        if bits & bit:
            place = place + bit - 2 * bit * lax.rem(lax.div(place, bit), 2)
        bit *= 2
    return place


def sum_kernel(devices, heads_ref, proj_ref, out_ref, w_buf, acc, *rest):
    stages = devices.bit_length() - 1
    sends, lands = rest[: stages + 1], rest[stages + 1 : 2 * stages + 1]
    w_sem, send_sem, recv_sem = rest[2 * stages + 1 :]
    place, section = lax.axis_index("sp"), lax.axis_index("section")
    sections = lax.axis_size("section")
    after = lax.rem(section + 1, sections)
    before = lax.rem(section + sections - 1, sections)
    rows = heads_ref.shape[0] // devices
    chunks = acc.shape[0]
    cols = acc.shape[2]
    mesh_id = pl.DeviceIdType.MESH
    partners = [(section, flipped(place, 1 << k)) for k in range(stages)]

    first_fetch = pltpu.make_async_copy(proj_ref.at[0, :, pl.ds(0, cols)], w_buf.at[0], w_sem.at[0])
    first_fetch.start()
    barrier = pltpu.get_barrier_semaphore()
    for other in partners + [(before, place)]:
        pl.semaphore_signal(barrier, inc=1, device_id=other, device_id_type=mesh_id)
    pl.semaphore_wait(barrier, stages + 1)

    def columns(t):
        return pl.ds(pl.multiple_of(t * cols, cols), cols)

    def fetch(t):
        slot = lax.rem(t, 2)
        return pltpu.make_async_copy(proj_ref.at[0, :, columns(t)], w_buf.at[slot], w_sem.at[slot])

    def move(k, t):
        return pltpu.make_async_remote_copy(
            src_ref=sends[k].at[t],
            dst_ref=lands[k].at[t] if k < stages else out_ref.at[:, columns(t)],
            send_sem=send_sem.at[k, t],
            recv_sem=recv_sem.at[k, t],
            device_id=partners[k] if k < stages else (after, place),
            device_id_type=mesh_id,
        )

    def product(t, flips):
        start = pl.multiple_of(flipped(place, flips) * rows, 16)
        return jnp.dot(
            heads_ref[pl.ds(start, rows), :], w_buf[lax.rem(t, 2)], preferred_element_type=jnp.float32
        )

    def multiply(t):
        fetch(t).wait()

        @pl.when(t + 1 < chunks)
        def _():
            fetch(t + 1).start()

        for i in range(devices // 2):
            sends[0][t, i * rows : (i + 1) * rows] = product(t, 2 * i + 1).astype(jnp.bfloat16)
        move(0, t).start()
        for i in range(devices // 2):
            acc[t, i * rows : (i + 1) * rows] = product(t, 2 * i)

    def combine(k, t):
        move(k, t).wait_recv()
        count = devices >> (k + 1)
        for i in range(count):
            spot = i << k
            summed = acc[t, spot * rows : (spot + 1) * rows] + lands[k][
                t, i * rows : (i + 1) * rows
            ].astype(jnp.float32)
            if i % 2 or count == 1:
                j = i // 2
                sends[k + 1][t, j * rows : (j + 1) * rows] = summed.astype(jnp.bfloat16)
            else:
                acc[t, spot * rows : (spot + 1) * rows] = summed
        move(k + 1, t).start()

    def step(t, carry):
        @pl.when(t < chunks)
        def _():
            multiply(t)

        for k in range(stages):
            done = t - LAG * (k + 1)

            @pl.when((done >= 0) & (done < chunks))
            def _():
                combine(k, done)

        return carry

    lax.fori_loop(0, chunks + LAG * stages, step, 0)

    def finish(t, carry):
        move(stages, t).wait_recv()
        for k in range(stages + 1):
            move(k, t).wait_send()
        return carry

    lax.fori_loop(0, chunks, finish, 0)


def summed_and_moved(heads_all, out_proj, devices):
    width, model = out_proj.shape[1], out_proj.shape[2]
    rows = TOKS // devices
    chunks = model // COLS
    stages = devices.bit_length() - 1
    sizes = [max(devices >> (k + 1), 1) * rows for k in range(stages + 1)]
    return pl.pallas_call(
        lambda *refs: sum_kernel(devices, *refs),
        out_shape=jax.ShapeDtypeStruct((rows, model), jnp.bfloat16),
        in_specs=[pl.BlockSpec(memory_space=pltpu.VMEM), pl.BlockSpec(memory_space=pl.ANY)],
        out_specs=pl.BlockSpec(memory_space=pl.ANY),
        scratch_shapes=[
            pltpu.VMEM((2, width, COLS), jnp.bfloat16),
            pltpu.VMEM((chunks, sizes[0], COLS), jnp.float32),
        ]
        + [pltpu.VMEM((chunks, size, COLS), jnp.bfloat16) for size in sizes]
        + [pltpu.VMEM((chunks, size, COLS), jnp.bfloat16) for size in sizes[:-1]]
        + [
            pltpu.SemaphoreType.DMA((2,)),
            pltpu.SemaphoreType.DMA((stages + 1, chunks)),
            pltpu.SemaphoreType.DMA((stages + 1, chunks)),
        ],
        compiler_params=pltpu.CompilerParams(
            collective_id=0, has_side_effects=True, vmem_limit_bytes=58 * 1024 * 1024
        ),
        cost_estimate=pl.CostEstimate(
            flops=2 * TOKS * width * model, bytes_accessed=2 * width * model, transcendentals=0
        ),
    )(heads_all, out_proj)


def rows_gathered(cut, rows, place, group):
    piece = cut(place)
    whole = jnp.zeros(piece.shape[:-2] + (rows * group, piece.shape[-1]), piece.dtype)
    lead = (0,) * (piece.ndim - 2)
    for bit in range(group):
        other = place ^ bit
        piece = cut(other)
        if bit:
            piece = swapped(piece, "sp", bit)
        whole = lax.dynamic_update_slice(whole, piece, (*lead, other % group * rows, 0))
    return whole


def both_videos(own, other, video):
    whole = jnp.zeros((TOKS, own.shape[1]), own.dtype)
    whole = lax.dynamic_update_slice(whole, own, (video * SPAN, 0))
    return lax.dynamic_update_slice(whole, other, ((1 - video) * SPAN, 0))


def per_device(resid, qkv, cache_kv, out_proj, gate, span_ids, cache_counts, span_mask):
    own_rows = resid.shape[1]
    width = cache_kv.shape[4]
    heads = width // HDIM
    devices = lax.axis_size("sp")
    group = devices // VIDS
    place = lax.axis_index("sp")
    video = place // group
    live_slots = visible_slots(span_ids[0], cache_counts[0], span_mask)

    def gathered(across, parts, source):
        def cut(other):
            holder = other ^ group if across else other
            begin, size = (0, holder * width), (own_rows, width)
            cuts = [lax.dynamic_slice(source[0, :, i], begin, size) for i in parts]
            return cuts[0] if len(cuts) == 1 else jnp.stack(cuts)

        return rows_gathered(cut, own_rows, place, group)

    across_q = gathered(True, (0,), qkv)
    own_q = gathered(False, (0,), qkv)
    other_q = swapped(across_q, "sp", group)
    source, _ = lax.optimization_barrier((qkv, across_q))
    across_kv = gathered(True, (1, 2), source)
    source, _ = lax.optimization_barrier((qkv, across_kv))
    own_kv = gathered(False, (1, 2), source)

    across_out, across_level = near_mix(across_q, across_kv)
    other_out = swapped(across_out, "sp", group)
    other_level = swapped(across_level[:, :heads].T, "sp", group).T
    other_level = jnp.pad(other_level, ((0, 0), (0, HDIM - heads)))

    queries = both_videos(own_q, other_q, video)
    queries, _ = lax.optimization_barrier((queries, across_out))
    far, far_level = far_mix(queries, cache_kv, live_slots)
    own_out, own_level = near_mix(own_q, own_kv)
    near = both_videos(own_out, other_out, video)
    near_level = both_videos(own_level, other_level, video)
    heads_all = join(far, far_level, near, near_level)

    resid_late, gate_late, _ = lax.optimization_barrier((resid, gate, heads_all))
    resid_prev = passed_along(resid_late[0], "section", 1)
    gate_prev = passed_along(gate_late[0], "section", 1)
    moved = summed_and_moved(heads_all, out_proj, devices).astype(jnp.float32)
    video_of = (place * own_rows + jnp.arange(own_rows, dtype=jnp.int32)) // SPAN
    gains = jnp.where((video_of == 0)[:, None], gate_prev[0:1], gate_prev[1:2])
    return (resid_prev + gains * moved)[None]


def solution(mesh):
    in_specs = (
        P("section", "sp", None),
        P("section", "sp", None, None),
        P("section", None, None, None, "sp"),
        P("section", "sp", None),
        P("section", None, None),
        P("section"),
        P("section"),
        P(),
    )
    out_specs = P("section", "sp", None)
    return jax.shard_map(
        per_device, mesh=mesh, in_specs=in_specs, out_specs=out_specs, check_vma=False
    )
```
